32 devices in a mesh: body: 4 (over y, x), dom: 8 (over z, core).
Axes of the slice: x: 2, y: 2, z: 4, core: 2. Of those that a mesh axis runs over, the one named last changes fastest.
Arguments:
- master_basis: bfloat16 [16384, 16, 256], P(('body', 'dom')), may hold values from -1.5 to 1.5
- master_weights: bfloat16 [16384, 4, 16], P(('body', 'dom')), may hold values from 0.099609375 to 1
- master_dest: int32 [16384, 1], P(('body', 'dom')), may hold values from 0 to 7; in each aligned block of 512 rows (0 to 511, 512 to 1023, ...) at most 128 rows name the same one
- master_slaves: int32 [16384, 4], P(('body', 'dom')), may hold values from 0 to 511
- slave_basis: bfloat16 [16384, 16, 256], P(('body', 'dom')), may hold values from -1.5 to 1.5
- slave_gain: float32 [16384], P(('body', 'dom')), may hold values from 0.1 to 1
- tile_owner: int32 [1024, 1], P(('body', 'dom')), may hold values from 0 to 7; in each aligned block of 32 rows (0 to 31, 32 to 63, ...) at most 8 rows name the same one
- tile_row: int32 [1024], P(('body', 'dom')), may hold values from 0 to 15
Outputs:
- coupling: float32 [512, 256, 256], P(('body', 'dom'))
The draws below stay inside these ranges and needn't reach their ends.
Inputs may be any that keep to these rules, and one draw needn't show every extreme that they name: `master_dest`: among the master segments of one device at most 128 name the same dom index, and that many is reached. `tile_owner`: among the tiles of one device at most 8 name the same owner, and that many is reached.
All inputs are finite; a program needn't handle non-finite values.
Results may differ from the reference program's by a relative error of at most 0.0027.
Values may be sent and summed in bfloat16 or wider, within the bound.
A program may use at most 256 MiB of HBM per device.

```python
import math
import jax
import jax.numpy as jnp
import numpy as np
from jax import lax

NP = 256
Q = 16
PAIRS = 4
SEG_DEV = 512
SLV_DEV = 512
TILE_DEV = 32
BR = 16
CAP = 128
TCAP = 8
SEGS = 16384
SLAVES = 16384
TILES = 1024
ROWS = 512
N_BODY = 4
N_DOM = 8


def place_ends(array, key, low, high):
    longest = array.shape.index(max(array.shape))
    spots = []
    for shift in (0, 1):
        where = [jax.random.randint(jax.random.fold_in(key, axis), (), 0, length) for axis, length in enumerate(array.shape)]
        where[longest] = (where[longest] + shift) % array.shape[longest]
        spots.append(tuple(where))
    return array.at[spots[0]].set(low).at[spots[1]].set(high)


def level_of(stream_key, extent, shards, least, top_value):
    loudness, own = 1.0, jax.random.fold_in(stream_key, 6)
    for dim, parts in shards:
        draws = jnp.exp(jax.random.uniform(jax.random.fold_in(own, dim), (parts,), jnp.float32, least / len(shards), top_value / len(shards)))
        loudness = loudness * jnp.repeat(draws, extent[dim] // parts).reshape([-1 if axis == dim else 1 for axis in range(len(extent))])
    return loudness


def deal_out(stream_key, own, number, rows, amount, top, bound, lean):
    order = jax.random.permutation(stream_key, amount)
    heavy_load, common = load_shares(amount, rows * top, bound, lean, True), load_shares(amount, rows * top, bound, lean, False)
    places = jnp.arange(amount)

    def named(tallies, rotation):
        used = int((tallies > 0).sum())
        fixed = max(1, used // 4)
        moved = fixed + (places - fixed + rotation * (used - fixed)) % max(1, amount - fixed)
        return jnp.zeros((amount,), jnp.int32).at[order[jnp.where(places < fixed, places, moved)]].set(jnp.asarray(tallies, jnp.int32))

    tallies = jnp.where(number % 4 == 0, named(heavy_load, number // 4), named(common, number - number // 4 - 1))
    mixed = jax.random.permutation(jax.random.fold_in(own, 3), amount)
    source_of, taker = mixed[0:amount // 2 * 2:2], mixed[1:amount // 2 * 2:2]
    margin = jnp.minimum(tallies[source_of] - 1, bound - tallies[taker]) // 2
    margin = jnp.where((source_of == order[0]) | (taker == order[0]) | (tallies[taker] == 0), 0, jnp.maximum(margin, 0))
    moved = jax.random.randint(jax.random.fold_in(own, 4), (amount // 2,), 0, 1 << 20) % (margin + 1)
    tallies = tallies.at[source_of].add(-moved).at[taker].add(moved)
    items = jnp.searchsorted(jnp.cumsum(tallies), jnp.arange(rows * top), side="right").astype(jnp.int32)
    grid = items.reshape(top, rows).T
    grid = grid[jax.random.permutation(jax.random.fold_in(own, 1), rows)]
    rotation = jax.random.randint(jax.random.fold_in(own, 2), (rows, 1), 0, top)
    return jnp.take_along_axis(grid, (jnp.arange(top)[None, :] + rotation) % top, axis=1)


def load_shares(number_of, total, bound, skew, full):
    loads = [(1 << 20) // math.isqrt(rank ** skew) + 1 for rank in range(1, number_of + 1)]
    largest = bound if full else min(bound, max(-(-total // number_of), total * loads[0] // sum(loads)))
    least = 1 if total - largest >= number_of - 1 else 0
    holding, rest = [largest] + [least] * (number_of - 1), total - largest - least * (number_of - 1)
    while rest > 0:
        candidates = [i for i in range(1, number_of) if holding[i] < largest] or [i for i in range(1, number_of) if holding[i] < bound]
        mass, left = sum([loads[i] for i in candidates]), rest
        for i in candidates:
            more = min(bound - holding[i], max(1, left * loads[i] // mass), rest)
            holding[i] = holding[i] + more
            rest = rest - more
    return np.array(holding)


def noise(key, extent, width, limit, cuts=(), held_as=jnp.bfloat16):
    drawn = jax.random.normal(key, extent, jnp.float32) * width
    if len(cuts) > 0:
        drawn = level_of(key, extent, cuts, -0.22, 0.18) * drawn
    return jnp.clip(drawn, min=-limit, max=limit).astype(held_as)


def setup_inputs(seed: int = 0) -> dict:
    splits = jax.random.split(jax.random.key(seed), 9)
    master_basis = noise(splits[0], (SEGS, Q, NP), 0.25, 1.5, ((0, 32),))
    master_weights = jnp.clip(jnp.exp(math.log(1.0) - 2.306499 * jax.random.uniform(splits[1], (SEGS, PAIRS, Q), jnp.float32) ** level_of(splits[1], (SEGS, PAIRS, Q), ((0, 32),), -0.2, 0.2)), 0.099609375, 1.0).astype(jnp.bfloat16)
    master_dest_keys = jax.random.split(jax.random.fold_in(splits[2], 1), SEGS // SEG_DEV)
    master_dest_turns = jax.random.permutation(jax.random.fold_in(splits[2], 3), SEGS // SEG_DEV)
    master_dest = jax.vmap(lambda own, number: deal_out(jax.random.fold_in(splits[2], 2), own, number, SEG_DEV, N_DOM, 1, CAP, 2))(master_dest_keys, master_dest_turns).reshape((SEGS, 1))
    master_slaves = place_ends(jax.random.randint(splits[3], (SEGS, PAIRS), 0, SLV_DEV), jax.random.fold_in(splits[3], 1), 0, SLV_DEV - 1).astype(jnp.int32)
    slave_basis = noise(splits[4], (SLAVES, Q, NP), 0.25, 1.5, ((0, 32),))
    slave_gain = jnp.clip(jnp.exp(math.log(1.0) - 2.3025851 * jax.random.uniform(splits[5], (SLAVES,), jnp.float32) ** level_of(splits[5], (SLAVES,), ((0, 32),), -0.2, 0.2)), 0.1, 1.0)
    tile_owner_keys = jax.random.split(jax.random.fold_in(splits[6], 1), TILES // TILE_DEV)
    tile_owner_turns = jax.random.permutation(jax.random.fold_in(splits[6], 3), TILES // TILE_DEV)
    tile_owner = jax.vmap(lambda own, number: deal_out(jax.random.fold_in(splits[6], 2), own, number, TILE_DEV, N_DOM, 1, TCAP, 2))(tile_owner_keys, tile_owner_turns).reshape((TILES, 1))
    tile_row = place_ends(jax.random.randint(splits[7], (TILES,), 0, BR), jax.random.fold_in(splits[7], 1), 0, BR - 1).astype(jnp.int32)
    return {"master_basis": master_basis, "master_weights": master_weights, "master_dest": master_dest, "master_slaves": master_slaves, "slave_basis": slave_basis, "slave_gain": slave_gain, "tile_owner": tile_owner, "tile_row": tile_row}


def reference(master_basis, master_weights, master_dest, master_slaves, slave_basis, slave_gain, tile_owner, tile_row):
    body_count = N_BODY
    dom_count = N_DOM
    source_dev = (jnp.arange(SEGS, dtype=jnp.int32) // SEG_DEV).astype(jnp.int32)
    target_dev = ((source_dev // dom_count + 1) % body_count) * dom_count + master_dest[:, 0]
    slave_global = (target_dev[:, None] * SLV_DEV + master_slaves).astype(jnp.int32)

    def add_block(block, carry):
        far_sum, weight_sum = carry
        first_row = (block * SEG_DEV).astype(jnp.int32)
        basis_rows = lax.dynamic_slice_in_dim(master_basis, first_row, SEG_DEV, 0).astype(jnp.float32)
        weights = lax.dynamic_slice_in_dim(master_weights, first_row, SEG_DEV, 0).astype(jnp.float32)
        slot_index = lax.dynamic_slice_in_dim(slave_global, first_row, SEG_DEV, 0).reshape(-1)
        weighted = weights[:, :, :, None] * basis_rows[:, None, :, :]
        far_sum = far_sum.at[slot_index].add(weighted.reshape(-1, Q, NP))
        weight_sum = weight_sum.at[slot_index].add(weights.reshape(-1, Q))
        return far_sum, weight_sum

    far_sum = jnp.zeros((SLAVES, Q, NP), jnp.float32)
    weight_sum = jnp.zeros((SLAVES, Q), jnp.float32)
    far_sum, weight_sum = lax.fori_loop(0, body_count * dom_count, add_block, (far_sum, weight_sum))
    slave_values = slave_basis.astype(jnp.float32)
    flux = ((slave_gain[:, None] + weight_sum)[:, :, None] * slave_values - far_sum).astype(jnp.bfloat16)
    per_tile = SLV_DEV // TILE_DEV
    left = slave_values.reshape(TILES, per_tile * Q, NP)
    right = flux.astype(jnp.float32).reshape(TILES, per_tile * Q, NP)
    coupling_tiles = jnp.einsum("tkn,tkm->tnm", left, right).astype(jnp.bfloat16)
    tile_dev = (jnp.arange(TILES, dtype=jnp.int32) // TILE_DEV).astype(jnp.int32)
    dest_row = ((tile_dev // dom_count) * dom_count + tile_owner[:, 0]) * BR + tile_row
    coupling = jnp.zeros((ROWS, NP, NP), jnp.float32).at[dest_row].add(coupling_tiles.astype(jnp.float32))
    return coupling
```

```python
import jax
import jax.numpy as jnp
from jax import lax
from jax.sharding import PartitionSpec as P

BR = 16
DIGIT = 32
LANES = 128


def shifted(block, axis, distance):
    devices = range(lax.axis_size(axis))
    route = [((i - distance) % len(devices), i) for i in devices]
    return lax.ppermute(block, axis, route)


def place_rows(target, groups, capacity):
    count = target.shape[0]
    index = jnp.arange(count, dtype=jnp.int32)
    earlier = (target[:, None] == target[None, :]) & (index[:, None] < index[None, :])
    position = jnp.sum(earlier.astype(jnp.int32), axis=0)
    slot_index = target * capacity + position
    slots = jnp.arange(groups * capacity, dtype=jnp.int32)
    return (slot_index[None, :] == slots[:, None]).astype(jnp.bfloat16)


def exchanged(block):
    return lax.all_to_all(block, "dom", split_axis=0, concat_axis=0, tiled=True)


def row_sums(owner, row, tiles, wanted):
    picks = (owner[None, :] == wanted) & (row[None, :] == jnp.arange(BR, dtype=jnp.int32)[:, None])
    return jnp.einsum(
        "jt,tnm->jnm", picks.astype(jnp.bfloat16), tiles, preferred_element_type=jnp.float32
    )


def assembled_by_chain(owner, row, tiles, chips):
    me = lax.axis_index("dom")
    total = row_sums(owner, row, tiles, me)
    for way in (1, -1):
        got = None
        for far in range(chips - 1, 0, -1):
            part = row_sums(owner, row, tiles, me + 2 * way * far)
            if got is not None:
                part = part + got.astype(jnp.float32)
            route = [
                (2 * z + core, 2 * (z + way) + core)
                for z in range(chips)
                if 0 <= z + way * far < chips
                for core in range(2)
            ]
            got = lax.ppermute(part.astype(jnp.bfloat16), "dom", route)
        total = total + got.astype(jnp.float32)
    return total


def assembled_by_exchange(owner, row, tiles, dom_count):
    count = tiles.shape[0]
    capacity = max(2, 2 * count // dom_count)
    placer = place_rows(owner, dom_count, capacity)
    packed = jnp.einsum("gt,tnm->gnm", placer, tiles, preferred_element_type=jnp.float32)
    rows = jnp.sum(placer.astype(jnp.int32) * (row + 1)[None, :], axis=1) - 1
    got_tiles = exchanged(packed.astype(jnp.bfloat16))
    got_rows = exchanged(rows)
    picks = (got_rows[None, :] == jnp.arange(BR, dtype=jnp.int32)[:, None]).astype(jnp.bfloat16)
    return jnp.einsum("jt,tnm->jnm", picks, got_tiles, preferred_element_type=jnp.float32)


def on_device(
    master_basis,
    master_weights,
    master_dest,
    master_slaves,
    slave_basis,
    slave_gain,
    tile_owner,
    tile_row,
):
    dom_count = lax.axis_size("dom")
    seg_count, quads, width = master_basis.shape
    pairs = master_slaves.shape[1]
    capacity = 2 * seg_count // dom_count
    slave_count = slave_basis.shape[0]
    tile_count = tile_row.shape[0]
    per_tile = slave_count // tile_count
    chips = dom_count // 2

    side = jnp.concatenate(
        [
            master_weights.reshape(seg_count, -1),
            (master_slaves // DIGIT).astype(jnp.bfloat16),
            (master_slaves % DIGIT).astype(jnp.bfloat16),
            master_dest.astype(jnp.bfloat16),
        ],
        axis=1,
    )
    side = jnp.pad(side, ((0, 0), (0, LANES - side.shape[1])))
    side = shifted(side, "body", 1)
    half = quads // 2
    by_quad = jnp.transpose(master_basis, (1, 0, 2))
    moved = []
    for column in range(0, width, LANES):
        for quad in (0, half):
            piece = by_quad[quad : quad + half, :, column : column + LANES]
            if moved:
                piece, _ = lax.optimization_barrier((piece, moved[-1]))
            moved.append(shifted(piece, "body", 1))

    fixed = pairs * quads
    dest = side[:, fixed + 2 * pairs].astype(jnp.int32)
    placer = place_rows(dest, dom_count, capacity)
    packed_side = jnp.dot(placer, side, preferred_element_type=jnp.float32).astype(jnp.bfloat16)
    got_side = exchanged(packed_side)
    packs = placer.reshape(dom_count, capacity, seg_count)
    got = []
    for piece in moved:
        packed = jnp.einsum(
            "gcr,qrn->gqcn", packs, piece, preferred_element_type=jnp.float32
        ).astype(jnp.bfloat16)
        got.append(exchanged(packed))

    weights = jnp.transpose(got_side[:, :fixed].astype(jnp.float32)).reshape(pairs, quads, -1)
    digits = jnp.transpose(got_side[:, fixed : fixed + 2 * pairs].astype(jnp.int32))
    owners = digits[:pairs] * DIGIT + digits[pairs:]
    local = jnp.arange(slave_count, dtype=jnp.int32)
    table = 0.0
    for p in range(pairs):
        match = local[:, None] == owners[p][None, :]
        table = table + jnp.where(match[None], weights[p][:, None, :], 0.0)
    high = lax.reduce_precision(table, 8, 7)
    low = (table - high).astype(jnp.bfloat16)
    high = high.astype(jnp.bfloat16)
    scale = slave_gain[None, :] + jnp.sum(table, axis=2)

    slave_quad = jnp.transpose(slave_basis, (1, 0, 2))
    owner, row = tile_owner[:, 0], tile_row
    if chips <= 4:
        swap = [(d, d ^ 1) for d in range(dom_count)]
        other = lax.ppermute(jnp.stack([owner, row]), "dom", swap)
        owner = jnp.concatenate([owner, other[0]])
        row = jnp.concatenate([row, other[1]])
    columns = []
    for index, column in enumerate(range(0, width, LANES)):
        tiles = 0.0
        for part, quad in enumerate((0, half)):
            rows = jnp.transpose(got[2 * index + part], (1, 0, 2, 3))
            rows = rows.reshape(half, dom_count * capacity, LANES)
            span = slice(quad, quad + half)
            far = jnp.einsum("qsr,qrn->qsn", high[span], rows, preferred_element_type=jnp.float32)
            far += jnp.einsum("qsr,qrn->qsn", low[span], rows, preferred_element_type=jnp.float32)
            own = slave_quad[span]
            near = own[:, :, column : column + LANES].astype(jnp.float32)
            flux = (scale[span, :, None] * near - far).astype(jnp.bfloat16)
            tiles += jnp.einsum(
                "qtkn,qtkm->tnm",
                own.reshape(half, tile_count, per_tile, width),
                flux.reshape(half, tile_count, per_tile, LANES),
                preferred_element_type=jnp.float32,
            )
        tiles = tiles.astype(jnp.bfloat16)
        if chips <= 4:
            tiles = jnp.concatenate([tiles, lax.ppermute(tiles, "dom", swap)])
            columns.append(assembled_by_chain(owner, row, tiles, chips))
        else:
            columns.append(assembled_by_exchange(owner, row, tiles, dom_count))
    return jnp.concatenate(columns, axis=2)


def solution(mesh):
    return jax.shard_map(
        on_device,
        mesh=mesh,
        in_specs=(
            P(("body", "dom"), None, None),
            P(("body", "dom"), None, None),
            P(("body", "dom"), None),
            P(("body", "dom"), None),
            P(("body", "dom"), None, None),
            P(("body", "dom")),
            P(("body", "dom"), None),
            P(("body", "dom")),
        ),
        out_specs=P(("body", "dom"), None, None),
        check_vma=False,
    )
```

```python
import jax
import jax.numpy as jnp
from jax import lax
from jax.sharding import PartitionSpec as P

BR = 16
DIGIT = 32
LANES = 128


def shifted(block, axis, distance):
    devices = range(lax.axis_size(axis))
    route = [((i - distance) % len(devices), i) for i in devices]
    return lax.ppermute(block, axis, route)


def place_rows(target, groups, capacity):
    count = target.shape[0]
    index = jnp.arange(count, dtype=jnp.int32)
    earlier = (target[:, None] == target[None, :]) & (index[:, None] < index[None, :])
    position = jnp.sum(earlier.astype(jnp.int32), axis=0)
    slot_index = target * capacity + position
    slots = jnp.arange(groups * capacity, dtype=jnp.int32)
    return (slot_index[None, :] == slots[:, None]).astype(jnp.bfloat16)


def exchanged(block):
    return lax.all_to_all(block, "dom", split_axis=0, concat_axis=0, tiled=True)


def row_sums(keys, sets, wanted):
    total = 0.0
    for (owner, row), tiles in zip(keys, sets):
        picks = (owner[None, :] == wanted) & (
            row[None, :] == jnp.arange(BR, dtype=jnp.int32)[:, None]
        )
        total += jnp.einsum(
            "jt,tnm->jnm", picks.astype(jnp.bfloat16), tiles, preferred_element_type=jnp.float32
        )
    return total


def chain_parts(keys, sets, chips, far, got):
    me = lax.axis_index("dom")
    parts = []
    for side, way in enumerate((1, -1)):
        part = row_sums(keys, sets, me + 2 * way * far)
        if got is not None:
            part = part + got[side].astype(jnp.float32)
        parts.append(part.astype(jnp.bfloat16))
    return parts


def chain_step(parts, chips, far):
    got = []
    for part, way in zip(parts, (1, -1)):
        route = [
            (2 * z + core, 2 * (z + way) + core)
            for z in range(chips)
            if 0 <= z + way * far < chips
            for core in range(2)
        ]
        got.append(lax.ppermute(part, "dom", route))
    return got


def finished(keys, sets, chips, far, parts):
    got = chain_step(parts, chips, far)
    for nearer in range(far - 1, 0, -1):
        got = chain_step(chain_parts(keys, sets, chips, nearer, got), chips, nearer)
    own = row_sums(keys, sets, lax.axis_index("dom"))
    return own + got[0].astype(jnp.float32) + got[1].astype(jnp.float32)


def tied(value, others):
    return lax.optimization_barrier((value, tuple(others)))[0]


def assembled_by_exchange(owner, row, tiles, dom_count):
    count = tiles.shape[0]
    capacity = max(2, 2 * count // dom_count)
    placer = place_rows(owner, dom_count, capacity)
    packed = jnp.einsum("gt,tnm->gnm", placer, tiles, preferred_element_type=jnp.float32)
    rows = jnp.sum(placer.astype(jnp.int32) * (row + 1)[None, :], axis=1) - 1
    got_tiles = exchanged(packed.astype(jnp.bfloat16))
    got_rows = exchanged(rows)
    picks = (got_rows[None, :] == jnp.arange(BR, dtype=jnp.int32)[:, None]).astype(jnp.bfloat16)
    return jnp.einsum("jt,tnm->jnm", picks, got_tiles, preferred_element_type=jnp.float32)


def on_device(
    master_basis,
    master_weights,
    master_dest,
    master_slaves,
    slave_basis,
    slave_gain,
    tile_owner,
    tile_row,
):
    dom_count = lax.axis_size("dom")
    seg_count, quads, width = master_basis.shape
    pairs = master_slaves.shape[1]
    capacity = 2 * seg_count // dom_count
    slave_count = slave_basis.shape[0]
    tile_count = tile_row.shape[0]
    per_tile = slave_count // tile_count
    chips = dom_count // 2

    side = jnp.concatenate(
        [
            master_weights.reshape(seg_count, -1),
            (master_slaves // DIGIT).astype(jnp.bfloat16),
            (master_slaves % DIGIT).astype(jnp.bfloat16),
            master_dest.astype(jnp.bfloat16),
        ],
        axis=1,
    )
    side = jnp.pad(side, ((0, 0), (0, LANES - side.shape[1])))
    side = shifted(side, "body", 1)
    half = quads // 2
    by_quad = jnp.transpose(master_basis, (1, 0, 2))
    moved = []
    for column in range(0, width, LANES):
        for quad in (0, half):
            piece = by_quad[quad : quad + half, :, column : column + LANES]
            if moved:
                piece, _ = lax.optimization_barrier((piece, moved[-1]))
            moved.append(shifted(piece, "body", 1))

    fixed = pairs * quads
    dest = side[:, fixed + 2 * pairs].astype(jnp.int32)
    placer = place_rows(dest, dom_count, capacity)
    packed_side = jnp.dot(placer, side, preferred_element_type=jnp.float32).astype(jnp.bfloat16)
    got_side = exchanged(packed_side)
    packs = placer.reshape(dom_count, capacity, seg_count)

    def packed(piece):
        return jnp.einsum(
            "gcr,qrn->gqcn", packs, piece, preferred_element_type=jnp.float32
        ).astype(jnp.bfloat16)

    weights = jnp.transpose(got_side[:, :fixed].astype(jnp.float32)).reshape(pairs, quads, -1)
    digits = jnp.transpose(got_side[:, fixed : fixed + 2 * pairs].astype(jnp.int32))
    owners = digits[:pairs] * DIGIT + digits[pairs:]
    local = jnp.arange(slave_count, dtype=jnp.int32)
    table = 0.0
    for p in range(pairs):
        match = local[:, None] == owners[p][None, :]
        table = table + jnp.where(match[None], weights[p][:, None, :], 0.0)
    high = lax.reduce_precision(table, 8, 7)
    low = (table - high).astype(jnp.bfloat16)
    high, low = lax.optimization_barrier((high.astype(jnp.bfloat16), low))
    scale = slave_gain[None, :] + jnp.sum(table, axis=2)

    slave_quad = jnp.transpose(slave_basis, (1, 0, 2))
    owner, row = tile_owner[:, 0], tile_row
    keys = [(owner, row)]
    if chips <= 4:
        swap = [(d, d ^ 1) for d in range(dom_count)]
        other = lax.ppermute(jnp.stack([owner, row]), "dom", swap)
        keys.append((other[0], other[1]))

    def flux_tiles(rows, column, quad):
        rows = jnp.transpose(rows, (1, 0, 2, 3))
        rows = rows.reshape(half, dom_count * capacity, LANES)
        span = slice(quad, quad + half)
        far = jnp.einsum("qsr,qrn->qsn", high[span], rows, preferred_element_type=jnp.float32)
        far += jnp.einsum("qsr,qrn->qsn", low[span], rows, preferred_element_type=jnp.float32)
        own = slave_quad[span]
        near = own[:, :, column : column + LANES].astype(jnp.float32)
        flux = (scale[span, :, None] * near - far).astype(jnp.bfloat16)
        return jnp.einsum(
            "qtkn,qtkm->tnm",
            own.reshape(half, tile_count, per_tile, width),
            flux.reshape(half, tile_count, per_tile, LANES),
            preferred_element_type=jnp.float32,
        )

    last = len(moved) - 1
    got, columns, chain = [], [], None
    tiles = 0.0
    for index, piece in enumerate(moved):
        if index >= 2:
            piece = tied(piece, [got[index - 2]])
        pack = packed(piece)
        if chain is not None and index == last:
            pack = tied(pack, chain)
        got.append(exchanged(pack))
        if index == 0:
            continue
        ready = [index - 1] if index < last else [index - 1, index]
        for chunk in ready:
            rows = got[chunk]
            if chain is not None and chunk == last:
                step = chain_step(chain, chips, chips - 1)
                chain = chain_parts(keys, sets, chips, chips - 2, step)
                rows = tied(rows, chain)
            column, quad = LANES * (chunk // 2), half * (chunk % 2)
            tiles = tiles + flux_tiles(rows, column, quad)
            if chunk % 2 == 0:
                continue
            tiles = tiles.astype(jnp.bfloat16)
            if chips > 4 or chips < 3:
                columns.append(assembled_by_exchange(owner, row, tiles, dom_count))
            elif chunk < last:
                sets = [tiles, lax.ppermute(tiles, "dom", swap)]
                chain = chain_parts(keys, sets, chips, chips - 1, None)
            else:
                columns.append(finished(keys, sets, chips, chips - 2, chain))
                sets = [tiles, lax.ppermute(tiles, "dom", swap)]
                chain = chain_parts(keys, sets, chips, chips - 1, None)
                columns.append(finished(keys, sets, chips, chips - 1, chain))
            tiles = 0.0
    return jnp.concatenate(columns, axis=2)


def solution(mesh):
    return jax.shard_map(
        on_device,
        mesh=mesh,
        in_specs=(
            P(("body", "dom"), None, None),
            P(("body", "dom"), None, None),
            P(("body", "dom"), None),
            P(("body", "dom"), None),
            P(("body", "dom"), None, None),
            P(("body", "dom")),
            P(("body", "dom"), None),
            P(("body", "dom")),
        ),
        out_specs=P(("body", "dom"), None, None),
        check_vma=False,
    )
```

```python
import jax
import jax.numpy as jnp
from jax import lax
from jax.sharding import PartitionSpec as P

BR = 16
DIGIT = 32
LANES = 128


def shifted(block, axis, distance):
    devices = range(lax.axis_size(axis))
    route = [((i - distance) % len(devices), i) for i in devices]
    return lax.ppermute(block, axis, route)


def place_rows(target, groups, capacity):
    count = target.shape[0]
    index = jnp.arange(count, dtype=jnp.int32)
    earlier = (target[:, None] == target[None, :]) & (index[:, None] < index[None, :])
    position = jnp.sum(earlier.astype(jnp.int32), axis=0)
    slot_index = target * capacity + position
    slots = jnp.arange(groups * capacity, dtype=jnp.int32)
    return (slot_index[None, :] == slots[:, None]).astype(jnp.bfloat16)


def exchanged(block):
    return lax.all_to_all(block, "dom", split_axis=0, concat_axis=0, tiled=True)


def row_sums(keys, sets, wanted):
    total = 0.0
    for (owner, row), tiles in zip(keys, sets):
        picks = (owner[None, :] == wanted) & (
            row[None, :] == jnp.arange(BR, dtype=jnp.int32)[:, None]
        )
        total += jnp.einsum(
            "jt,tnm->jnm", picks.astype(jnp.bfloat16), tiles, preferred_element_type=jnp.float32
        )
    return total


def chain_parts(keys, sets, chips, far, got):
    me = lax.axis_index("dom")
    parts = []
    for side, way in enumerate((1, -1)):
        part = row_sums(keys, sets, me + 2 * way * far)
        if got is not None:
            part = part + got[side].astype(jnp.float32)
        parts.append(part.astype(jnp.bfloat16))
    return parts


def chain_step(parts, chips, far):
    got = []
    for part, way in zip(parts, (1, -1)):
        route = [
            (2 * z + core, 2 * (z + way) + core)
            for z in range(chips)
            if 0 <= z + way * far < chips
            for core in range(2)
        ]
        got.append(lax.ppermute(part, "dom", route))
    return got


def finished(keys, sets, chips, far, parts):
    got = chain_step(parts, chips, far)
    for nearer in range(far - 1, 0, -1):
        got = chain_step(chain_parts(keys, sets, chips, nearer, got), chips, nearer)
    own = row_sums(keys, sets, lax.axis_index("dom"))
    return own + got[0].astype(jnp.float32) + got[1].astype(jnp.float32)


def tied(value, others):
    return lax.optimization_barrier((value, tuple(others)))[0]


def assembled_by_exchange(owner, row, tiles, dom_count):
    count = tiles.shape[0]
    capacity = max(2, 2 * count // dom_count)
    placer = place_rows(owner, dom_count, capacity)
    packed = jnp.einsum("gt,tnm->gnm", placer, tiles, preferred_element_type=jnp.float32)
    rows = jnp.sum(placer.astype(jnp.int32) * (row + 1)[None, :], axis=1) - 1
    got_tiles = exchanged(packed.astype(jnp.bfloat16))
    got_rows = exchanged(rows)
    picks = (got_rows[None, :] == jnp.arange(BR, dtype=jnp.int32)[:, None]).astype(jnp.bfloat16)
    return jnp.einsum("jt,tnm->jnm", picks, got_tiles, preferred_element_type=jnp.float32)


def on_device(
    master_basis,
    master_weights,
    master_dest,
    master_slaves,
    slave_basis,
    slave_gain,
    tile_owner,
    tile_row,
):
    dom_count = lax.axis_size("dom")
    seg_count, quads, width = master_basis.shape
    pairs = master_slaves.shape[1]
    capacity = 2 * seg_count // dom_count
    slave_count = slave_basis.shape[0]
    tile_count = tile_row.shape[0]
    per_tile = slave_count // tile_count
    chips = dom_count // 2

    side = jnp.concatenate(
        [
            master_weights.reshape(seg_count, -1),
            (master_slaves // DIGIT).astype(jnp.bfloat16),
            (master_slaves % DIGIT).astype(jnp.bfloat16),
            master_dest.astype(jnp.bfloat16),
        ],
        axis=1,
    )
    side = jnp.pad(side, ((0, 0), (0, LANES - side.shape[1])))
    side = shifted(side, "body", 1)
    few = quads // 4
    pieces = [
        (column, start, stop)
        for column, cut in ((0, few), (LANES, quads - few))
        for start, stop in ((0, cut), (cut, quads))
    ]
    by_quad = jnp.transpose(master_basis, (1, 0, 2))
    moved = []
    for column, start, stop in pieces:
        piece = by_quad[start:stop, :, column : column + LANES]
        if moved:
            piece, _ = lax.optimization_barrier((piece, moved[-1]))
        moved.append(shifted(piece, "body", 1))

    fixed = pairs * quads
    dest = side[:, fixed + 2 * pairs].astype(jnp.int32)
    placer = place_rows(dest, dom_count, capacity)
    packed_side = jnp.dot(placer, side, preferred_element_type=jnp.float32).astype(jnp.bfloat16)
    got_side = exchanged(packed_side)
    packs = placer.reshape(dom_count, capacity, seg_count)

    def packed(piece):
        return jnp.einsum(
            "gcr,qrn->gqcn", packs, piece, preferred_element_type=jnp.float32
        ).astype(jnp.bfloat16)

    weights = jnp.transpose(got_side[:, :fixed].astype(jnp.float32)).reshape(pairs, quads, -1)
    digits = jnp.transpose(got_side[:, fixed : fixed + 2 * pairs].astype(jnp.int32))
    owners = digits[:pairs] * DIGIT + digits[pairs:]
    local = jnp.arange(slave_count, dtype=jnp.int32)
    table = 0.0
    for p in range(pairs):
        match = local[:, None] == owners[p][None, :]
        table = table + jnp.where(match[None], weights[p][:, None, :], 0.0)
    high = lax.reduce_precision(table, 8, 7)
    low = (table - high).astype(jnp.bfloat16)
    high, low = lax.optimization_barrier((high.astype(jnp.bfloat16), low))
    scale = slave_gain[None, :] + jnp.sum(table, axis=2)

    slave_quad = jnp.transpose(slave_basis, (1, 0, 2))
    owner, row = tile_owner[:, 0], tile_row
    keys = [(owner, row)]
    if chips <= 4:
        swap = [(d, d ^ 1) for d in range(dom_count)]
        other = lax.ppermute(jnp.stack([owner, row]), "dom", swap)
        keys.append((other[0], other[1]))

    def flux_tiles(rows, column, start, stop):
        depth = stop - start
        rows = jnp.transpose(rows, (1, 0, 2, 3))
        rows = rows.reshape(depth, dom_count * capacity, LANES)
        span = slice(start, stop)
        far = jnp.einsum("qsr,qrn->qsn", high[span], rows, preferred_element_type=jnp.float32)
        far += jnp.einsum("qsr,qrn->qsn", low[span], rows, preferred_element_type=jnp.float32)
        own = slave_quad[span]
        near = own[:, :, column : column + LANES].astype(jnp.float32)
        flux = (scale[span, :, None] * near - far).astype(jnp.bfloat16)
        return jnp.einsum(
            "qtkn,qtkm->tnm",
            own.reshape(depth, tile_count, per_tile, width),
            flux.reshape(depth, tile_count, per_tile, LANES),
            preferred_element_type=jnp.float32,
        )

    last = len(moved) - 1
    got, columns, chain = [], [], None
    tiles = 0.0
    for index, piece in enumerate(moved):
        if index >= 2:
            piece = tied(piece, [got[index - 2]])
        got.append(exchanged(packed(piece)))
        if index == 0:
            continue
        ready = [index - 1] if index < last else [index - 1, index]
        for chunk in ready:
            rows = got[chunk]
            if chain is not None and chunk < last:
                rows = tied(rows, chain)
            if chain is not None and chunk == last:
                step = chain_step(chain, chips, chips - 1)
                chain = chain_parts(keys, sets, chips, chips - 2, step)
                rows = tied(rows, chain)
            tiles = tiles + flux_tiles(rows, *pieces[chunk])
            if chunk % 2 == 0:
                continue
            tiles = tiles.astype(jnp.bfloat16)
            if chips > 4 or chips < 3:
                columns.append(assembled_by_exchange(owner, row, tiles, dom_count))
            elif chunk < last:
                sets = [tiles, lax.ppermute(tiles, "dom", swap)]
                chain = chain_parts(keys, sets, chips, chips - 1, None)
            else:
                columns.append(finished(keys, sets, chips, chips - 2, chain))
                sets = [tiles, lax.ppermute(tiles, "dom", swap)]
                chain = chain_parts(keys, sets, chips, chips - 1, None)
                columns.append(finished(keys, sets, chips, chips - 1, chain))
            tiles = 0.0
    return jnp.concatenate(columns, axis=2)


def solution(mesh):
    return jax.shard_map(
        on_device,
        mesh=mesh,
        in_specs=(
            P(("body", "dom"), None, None),
            P(("body", "dom"), None, None),
            P(("body", "dom"), None),
            P(("body", "dom"), None),
            P(("body", "dom"), None, None),
            P(("body", "dom")),
            P(("body", "dom"), None),
            P(("body", "dom")),
        ),
        out_specs=P(("body", "dom"), None, None),
        check_vma=False,
    )
```
